32 devices in a mesh: section: 4 (over y, core), expert: 8 (over z, x).
Axes of the slice: x: 2, y: 2, z: 4, core: 2. Of those that a mesh axis runs over, the one named last changes fastest.
Arguments:
- out_grad: bfloat16 [4, 1024, 7168], P('section', 'expert'), may hold values from -6 to 6
- router_weight: bfloat16 [4, 7168, 2], P('section'), may hold values from -0.25 to 0.25
- down_weight: bfloat16 [4, 2048, 7168], P('section', 'expert'), may hold values from -0.1875 to 0.1875
- hidden_saved: bfloat16 [4, 8, 8, 32, 256], P('section', 'expert'), may hold values from -1.5 to 1.5
- slot_token: int32 [4, 8, 2, 32], P('section', 'expert'), may hold values from 0 to 127, as said below
- slot_count: int32 [4, 8, 2], P('section', 'expert'), may hold values from 8 to 32, as said below
- slot_gate: float32 [4, 8, 2, 32], P('section', 'expert'), may hold values from 0.02 to 1
Outputs:
- down_grad: bfloat16 [4, 2048, 7168], P('section', 'expert')
- hidden_grad: bfloat16 [4, 8, 8, 32, 256], P('section', 'expert')
- passed_grad: bfloat16 [4, 1024, 7168], P('section', 'expert')
The draws below stay inside these ranges and needn't reach their ends.
Inputs may be any that keep to these rules, and one draw needn't show every extreme that they name: `slot_token`: within each block the used slots name distinct tokens; entries at slots from the count onward are ignored. `slot_count`: in every section one expert has 32 used slots in the block of every source device.
All inputs are finite; a program needn't handle non-finite values.
Results may differ from the reference program's by a relative error of at most 0.015.
Values may be sent and summed in bfloat16 or wider, within the bound.
A program may use at most 128 MiB of HBM per device.

```python
import math
import jax
import jax.numpy as jnp
from jax import lax

D = 7168
HID = 1024
GROUP = 4
TOK_DEV = 128
HID_DEV = 256
EXPERTS = 2
CAP = 32
TOKENS = 1024
N_SECTION = 4
N_EXPERT = 8


def draw_slot_token(key, part):
    inner = jax.random.fold_in(key, 11)
    keys = jax.random.split(inner, N_SECTION * N_EXPERT * EXPERTS)
    perms = jax.vmap(lambda k: jax.random.permutation(k, TOK_DEV))(keys)
    return perms[:, :CAP].reshape(N_SECTION, N_EXPERT, EXPERTS, CAP).astype(jnp.int32)


def draw_slot_count(key, part):
    inner = jax.random.fold_in(key, 23)
    first, second = jax.random.split(inner)
    counts = jax.random.randint(first, (N_SECTION, N_EXPERT, EXPERTS), CAP // 4, CAP + 1)
    hottest = jax.random.randint(second, (N_SECTION,), 0, EXPERTS)
    column = lax.broadcasted_iota(jnp.int32, (N_SECTION, N_EXPERT, EXPERTS), 2)
    return jnp.where(column == hottest[:, None, None], CAP, counts).astype(jnp.int32)


def steps_of(key, extent, shards, low, top_value):
    level = 1.0
    for dim, blocks in shards:
        steps = jax.random.uniform(jax.random.fold_in(jax.random.fold_in(key, 6), dim), (blocks,), jnp.float32, low / len(shards), top_value / len(shards))
        level = level * jnp.repeat(jnp.exp(steps), extent[dim] // blocks).reshape((-1,) + (1,) * (len(extent) - 1 - dim))
    return level


def scatter_about(rng, extent, width, bound, pieces=(), kind=jnp.bfloat16):
    result = jax.random.normal(rng, extent, jnp.float32) * width
    if len(pieces) > 0:
        result = steps_of(rng, extent, pieces, -0.22, 0.18) * result
    return jnp.clip(result, min=-bound, max=bound).astype(kind)


def setup_inputs(seed: int = 0) -> dict:
    key_list = jax.random.split(jax.random.key(seed), 8)
    return {
        "out_grad": scatter_about(key_list[0], (N_SECTION, TOKENS, D), 1.0, 6.0, ((0, 4), (1, 8))),
        "router_weight": scatter_about(key_list[1], (N_SECTION, D, EXPERTS), (D // 16) ** -0.5, 0.25, ((0, 4),)),
        "down_weight": scatter_about(key_list[2], (N_SECTION, EXPERTS * HID, D), HID ** -0.5, 0.1875, ((0, 4), (1, 8))),
        "hidden_saved": scatter_about(key_list[3], (N_SECTION, N_EXPERT, N_EXPERT, CAP, HID_DEV), 0.25, 1.5, ((0, 4), (1, 8))),
        "slot_token": draw_slot_token(jax.random.fold_in(key_list[7], 71), 0),
        "slot_count": draw_slot_count(jax.random.fold_in(key_list[7], 71), 0),
        "slot_gate": jnp.clip(jnp.exp(math.log(1.0) - 3.912023 * jax.random.uniform(key_list[6], (N_SECTION, N_EXPERT, EXPERTS, CAP), jnp.float32) ** steps_of(key_list[6], (N_SECTION, N_EXPERT, EXPERTS, CAP), ((0, 4), (1, 8)), -0.2, 0.2)), 0.02, 1.0),
    }


def section_pass(grad, router, weight, saved, tokens, counts, gates):
    high = lax.Precision.HIGHEST
    grad_src = grad.reshape(N_EXPERT, TOK_DEV, D)
    slots = lax.broadcasted_iota(jnp.int32, (N_EXPERT, EXPERTS, CAP), 2)
    live = slots < counts[:, :, None]
    gate_live = jnp.where(live, gates, jnp.float32(0.0)).astype(jnp.float32)
    rows = jax.vmap(lambda g, t: g[t])(grad_src, tokens)
    rows = jnp.where(live[..., None], rows, jnp.zeros((), jnp.bfloat16))
    blocks = weight.reshape(N_EXPERT, HID_DEV, D)

    def per_owner(owner):
        expert_id = (owner // GROUP).astype(jnp.int32)
        block_rows = lax.dynamic_index_in_dim(rows, expert_id, 1, keepdims=False)
        block_gate = lax.dynamic_index_in_dim(gate_live, expert_id, 1, keepdims=False)
        w_block = lax.dynamic_index_in_dim(blocks, owner, 0, keepdims=False)
        held = lax.dynamic_index_in_dim(saved, owner, 0, keepdims=False)
        proj = jnp.einsum("scd,hd->sch", block_rows.astype(jnp.float32), w_block.astype(jnp.float32), precision=high)
        grad_hidden = (block_gate[..., None] * proj).astype(jnp.bfloat16)
        partial_value = jnp.sum(held.astype(jnp.float32) * proj, axis=-1)
        scaled = (block_gate[..., None] * block_rows.astype(jnp.float32)).astype(jnp.bfloat16)
        w_grad = jnp.einsum("sch,scd->hd", held.astype(jnp.float32), scaled.astype(jnp.float32), precision=high)
        return w_grad.astype(jnp.bfloat16), grad_hidden, partial_value

    w_grads, hidden_grads, partials = lax.map(per_owner, jnp.arange(N_EXPERT, dtype=jnp.int32))
    gate_grad = partials.reshape(EXPERTS, GROUP, N_EXPERT, CAP).sum(axis=1)
    gate_grad = jnp.transpose(gate_grad, (1, 0, 2))
    positions = lax.broadcasted_iota(jnp.int32, (N_EXPERT, EXPERTS, CAP, TOK_DEV), 3)
    match = jnp.where((tokens[..., None] == positions) & live[..., None], jnp.float32(1.0), jnp.float32(0.0))
    logit_grad = jnp.einsum("sec,sect->ste", gate_grad, match, precision=high).reshape(TOKENS, EXPERTS)
    input_grad = grad.astype(jnp.float32) + jnp.dot(logit_grad, router.astype(jnp.float32).T, precision=high)
    return w_grads.reshape(N_EXPERT * HID_DEV, D), hidden_grads, input_grad.astype(jnp.bfloat16)


def reference(out_grad, router_weight, down_weight, hidden_saved, slot_token, slot_count, slot_gate):
    down_grad, hidden_grad, input_grad = lax.map(
        lambda a: section_pass(*a),
        (out_grad, router_weight, down_weight, hidden_saved, slot_token, slot_count, slot_gate))
    zeros = jnp.zeros((1, TOKENS, D), jnp.bfloat16)
    passed_grad = jnp.concatenate([input_grad[1:], zeros], axis=0)
    return down_grad, hidden_grad, passed_grad
```

```python
import functools

import jax
import jax.numpy as jnp
from jax import lax
from jax.experimental import pallas as pl
from jax.experimental.pallas import tpu as pltpu
from jax.sharding import PartitionSpec as P

MESH = pl.DeviceIdType.MESH
F32 = jnp.float32
BF16 = jnp.bfloat16
CHUNK = 512
LEAD = 2


def exchange(
    sizes,
    tok_ref, cnt_ref, gate_ref, held_ref, router_ref, grad_hbm, w_hbm,
    scaled_hbm, held_t_ref, hg_ref, next_hbm, rnext_hbm, logit_ref,
    gradv, wv, buf, outbuf, scaledv, proj, onehot, gsend, grecv, gcol,
    tsend, trecv, rsend, psend, precv,
    s_out, s_own, s_fwd, s_diag, s_gate, s_next, s_small, s_part,
    r_blk, r_gate, r_next, r_small, r_part, l_grad, l_w, l_scaled,
):
    sections, owners, experts, cap, chunks = sizes
    group = owners // experts
    width = gradv.shape[2]
    toks = gradv.shape[1]
    sec = lax.axis_index("section")
    me = lax.axis_index("expert")
    mine = me // group
    member = lax.rem(me, group)
    hi, lo = member // 2, lax.rem(member, 2)
    far_m = (1 - hi) * 2 + lo
    side_m = hi * 2 + (1 - lo)
    diag_m = (1 - hi) * 2 + (1 - lo)

    def at_expert(index):
        return {"section": sec, "expert": index}

    def at_previous(index):
        return {"section": sec - 1, "expert": index}

    def in_group(r, m):
        return lax.rem(mine + r, experts) * group + m

    def block(source, c):
        return buf.at[c, pl.ds(pl.multiple_of(source * cap, cap), cap)]

    def grad_load(c):
        return pltpu.make_async_copy(
            grad_hbm.at[:, pl.ds(pl.multiple_of(c * width, width), width)], gradv.at[c], l_grad.at[c])

    def w_load(c):
        return pltpu.make_async_copy(
            w_hbm.at[:, pl.ds(pl.multiple_of(c * width, width), width)], wv.at[c], l_w.at[c])

    def scaled_store(c):
        return pltpu.make_async_copy(scaledv.at[c], scaled_hbm.at[c], l_scaled.at[c])

    def send(src, dst, s_sem, r_sem, device):
        return pltpu.make_async_remote_copy(
            src_ref=src, dst_ref=dst, send_sem=s_sem, recv_sem=r_sem,
            device_id=device, device_id_type=MESH)

    def out_copy(r, c):
        return send(outbuf.at[r - 1, c], block(me, c), s_out.at[r - 1, c], r_blk.at[me, c],
                    at_expert(in_group(r, member)))

    def relay(source, c, s_sem, m):
        return send(block(source, c), block(source, c), s_sem, r_blk.at[source, c],
                    at_expert(in_group(0, m)))

    def own_copy(side, c):
        return relay(me, c, s_own.at[side, c], side_m if side else far_m)

    def fwd_copy(r, side, c):
        return relay(in_group(r, member), c, s_fwd.at[r - 1, side, c], side_m if side else far_m)

    def diag_by_far(r, c):
        return relay(in_group(r, far_m), c, s_diag.at[r, c], side_m)

    def diag_by_side(r, c):
        return relay(in_group(r, side_m), c, s_diag.at[r, c], far_m)

    def got(source, c):
        relay(source, c, s_own.at[0, c], far_m).wait_recv()

    def next_copy(c):
        return send(gradv.at[c], next_hbm.at[c], s_next.at[c], r_next.at[c], at_previous(me))

    def router_copy():
        return send(rsend, rnext_hbm, s_small.at[0], r_small.at[0], at_previous(me))

    def token_copy():
        return send(tsend, trecv, s_small.at[1], r_small.at[1], at_previous(me))

    def gate_copy(r, q):
        return send(gsend.at[r], grecv.at[me], s_gate.at[r, q], r_gate.at[me],
                    at_expert(in_group(r, lax.rem(member + q, group))))

    def part_copy(i):
        return send(psend.at[i], precv.at[me], s_part.at[i], r_part.at[me], at_previous(i))

    gate_pairs = [(r, q) for r in range(experts) for q in range(group) if r or q]

    barrier = pltpu.get_barrier_semaphore()
    for step in range(1, owners):
        pl.semaphore_signal(barrier, inc=1, device_id=at_expert(lax.rem(me + step, owners)),
                            device_id_type=MESH)

    @pl.when(sec < sections - 1)
    def _():
        for i in range(owners):
            pl.semaphore_signal(barrier, inc=1, device_id={"section": sec + 1, "expert": i},
                                device_id_type=MESH)

    def start_grad(c, carry):
        grad_load(c).start()
        return carry

    def start_w(c, carry):
        w_load(c).start()
        return carry

    lax.fori_loop(0, chunks, start_grad, 0)
    lax.fori_loop(0, chunks, start_w, 0)

    eye = lax.broadcasted_iota(jnp.int32, (cap, cap), 0) == lax.broadcasted_iota(jnp.int32, (cap, cap), 1)
    slot = lax.broadcasted_iota(jnp.int32, (1, cap), 1)

    def column(row):
        return jnp.sum(jnp.where(eye, row, 0.0), axis=1, keepdims=True)

    def row_of(col):
        return jnp.sum(jnp.where(eye, col, 0.0), axis=0, keepdims=True)

    places = lax.broadcasted_iota(jnp.int32, (cap, toks), 1).astype(F32)
    gsend[...] = jnp.zeros_like(gsend)
    tsend[...] = jnp.full(tsend.shape, -1, jnp.int32)
    for r in range(experts):
        e = lax.rem(mine + r, experts)
        live = slot < cnt_ref[e]
        tok = jnp.where(live, tok_ref[pl.ds(e, 1), :], -1)
        hit = jnp.where(column(tok.astype(F32)) == places, 1.0, 0.0)
        onehot[r * cap:(r + 1) * cap, :] = hit.astype(BF16)
        gsend[r, 0:1, 0:cap] = jnp.where(live, gate_ref[pl.ds(e, 1), :], 0.0)
    for e in range(experts):
        tsend[e:e + 1, 0:cap] = jnp.where(slot < cnt_ref[e], tok_ref[e:e + 1, :], -1)
    grecv[me] = gsend[0]
    rsend[...] = jnp.zeros_like(rsend)
    rsend[0:experts, :] = router_ref[...]

    def gather(c):
        grad_load(c).wait()
        rows = lax.dot_general(onehot[...], gradv[c], (((1,), (0,)), ((), ())),
                               preferred_element_type=F32).astype(BF16)
        buf[c, pl.ds(pl.multiple_of(me * cap, cap), cap), :] = rows[:cap]
        for r in range(1, experts):
            outbuf[r - 1, c] = rows[r * cap:(r + 1) * cap]

    gather(0)
    pl.semaphore_wait(barrier, (owners - 1) + jnp.where(sec > 0, owners, 0))

    def step(t, carry):
        @pl.when(t < chunks)
        def _():
            for r in range(1, experts):
                out_copy(r, t).start()
            own_copy(0, t).start()
            own_copy(1, t).start()

            @pl.when(t + 1 < chunks)
            def _():
                gather(t + 1)

            @pl.when(sec > 0)
            def _():
                next_copy(t).start()

        @pl.when(t == 0)
        def _():
            for r, q in gate_pairs:
                gate_copy(r, q).start()

            @pl.when(sec > 0)
            def _():
                router_copy().start()
                token_copy().start()

        c1 = t - LEAD

        @pl.when((c1 >= 0) & (c1 < chunks))
        def _():
            for r in range(1, experts):
                got(in_group(r, member), c1)
                fwd_copy(r, 0, c1).start()
                fwd_copy(r, 1, c1).start()

        c2 = t - 2 * LEAD

        @pl.when((c2 >= 0) & (c2 < chunks))
        def _():
            for r in range(experts):
                got(in_group(r, far_m), c2)
                got(in_group(r, side_m), c2)
                side_first = lax.rem(c2 + 2 * r, 4) == 1

                @pl.when(side_first)
                def _():
                    diag_by_side(r, c2).start()

                @pl.when(jnp.logical_not(side_first))
                def _():
                    diag_by_far(r, c2).start()

        c3 = t - 3 * LEAD

        @pl.when(c3 == 0)
        def _():
            for i in range(1, owners):
                other = lax.rem(me + i, owners)
                send(gsend.at[0], grecv.at[other], s_gate.at[0, 1], r_gate.at[other],
                     at_expert(other)).wait_recv()
            for i in range(owners):
                gcol[i * cap:(i + 1) * cap, :] = jnp.broadcast_to(
                    column(grecv[i, 0:1, 0:cap]), (cap, gcol.shape[1]))
            held_t_ref[...] = held_ref[...].astype(F32).T.astype(BF16)
            proj[...] = jnp.zeros_like(proj)

        @pl.when(c3 >= 0)
        def _():
            for r in range(experts):
                got(in_group(r, diag_m), c3)
            w_load(c3).wait()
            proj[...] += lax.dot_general(buf[c3], wv[c3], (((1,), (1,)), ((), ())),
                                         preferred_element_type=F32)
            for p in range(0, width, 128):
                scaledv[c3, :, p:p + 128] = (gcol[...] * buf[c3, :, p:p + 128].astype(F32)).astype(BF16)
            scaled_store(c3).start()

        return carry

    lax.fori_loop(0, chunks + 3 * LEAD, step, 0)

    partial = jnp.sum(held_ref[...].astype(F32) * proj[...], axis=1, keepdims=True)
    psend[...] = jnp.zeros_like(psend)
    for i in range(owners):
        psend[i, 0:1, 0:cap] = row_of(partial[i * cap:(i + 1) * cap])

    @pl.when(sec > 0)
    def _():
        for i in range(owners):
            part_copy(i).start()

    hg_ref[...] = (gcol[:, 0:1] * proj[...]).astype(BF16)

    def drain(c, carry):
        for r in range(1, experts):
            out_copy(r, c).wait_send()
            fwd_copy(r, 0, c).wait_send()
            fwd_copy(r, 1, c).wait_send()
        own_copy(0, c).wait_send()
        own_copy(1, c).wait_send()
        for r in range(experts):
            diag_by_far(r, c).wait_send()

        @pl.when(sec > 0)
        def _():
            next_copy(c).wait_send()

        @pl.when(sec < sections - 1)
        def _():
            next_copy(c).wait_recv()

        scaled_store(c).wait()
        return carry

    lax.fori_loop(0, chunks, drain, 0)
    for r, q in gate_pairs:
        gate_copy(r, q).wait_send()

    logit_ref[...] = jnp.zeros_like(logit_ref)

    @pl.when(sec < sections - 1)
    def _():
        router_copy().wait_recv()
        token_copy().wait_recv()
        for j in range(owners):
            send(psend.at[j], precv.at[j], s_part.at[j], r_part.at[j], at_expert(j)).wait_recv()
        lane = lax.broadcasted_iota(jnp.int32, logit_ref.shape, 1)
        where_tok = lax.broadcasted_iota(jnp.int32, (toks, cap), 0)
        total = jnp.zeros(logit_ref.shape, F32)
        for e in range(experts):
            gate_grad = precv[e * group, 0:1, 0:cap]
            for q in range(1, group):
                gate_grad = gate_grad + precv[e * group + q, 0:1, 0:cap]
            match = where_tok == trecv[e:e + 1, 0:cap]
            col = jnp.sum(jnp.where(match, gate_grad, 0.0), axis=1, keepdims=True)
            total = jnp.where(lane == e, col, total)
        logit_ref[...] = total

    @pl.when(sec > 0)
    def _():
        router_copy().wait_send()
        token_copy().wait_send()
        for i in range(owners):
            part_copy(i).wait_send()


def finish(sections, experts, held_t_ref, scaled_ref, logit_ref, next_ref, router_ref, down_ref, passed_ref):
    down_ref[...] = jnp.dot(held_t_ref[...], scaled_ref[0], preferred_element_type=F32).astype(BF16)
    total = next_ref[0].astype(F32)
    for e in range(experts):
        total = total + logit_ref[:, e:e + 1] * router_ref[e:e + 1, :].astype(F32)
    last = lax.axis_index("section") == sections - 1
    passed_ref[...] = jnp.where(last, 0.0, total).astype(BF16)


def shards(out_grad, router_weight, down_weight, hidden_saved, slot_token, slot_count, slot_gate):
    sections, owners = lax.axis_size("section"), lax.axis_size("expert")
    grad, w_block = out_grad[0], down_weight[0]
    toks, width = grad.shape
    hid = w_block.shape[0]
    experts, cap = slot_token.shape[2:]
    group = owners // experts
    assert group == 4 and width % CHUNK == 0
    chunks = width // CHUNK
    slots = owners * cap
    pad_e = -(-experts // 8) * 8
    pad_r = -(-experts // 16) * 16
    held = hidden_saved.reshape(slots, hid)
    vmem = pl.BlockSpec(memory_space=pltpu.VMEM)
    smem = pl.BlockSpec(memory_space=pltpu.SMEM)
    anyw = pl.BlockSpec(memory_space=pl.ANY)
    dma = pltpu.SemaphoreType.DMA
    shape = jax.ShapeDtypeStruct
    scratch = [
        pltpu.VMEM((chunks, toks, CHUNK), BF16),
        pltpu.VMEM((chunks, hid, CHUNK), BF16),
        pltpu.VMEM((chunks, slots, CHUNK), BF16),
        pltpu.VMEM((experts - 1, chunks, cap, CHUNK), BF16),
        pltpu.VMEM((chunks, slots, CHUNK), BF16),
        pltpu.VMEM((slots, hid), F32),
        pltpu.VMEM((experts * cap, toks), BF16),
        pltpu.VMEM((experts, 8, 128), F32),
        pltpu.VMEM((owners, 8, 128), F32),
        pltpu.VMEM((slots, 128), F32),
        pltpu.VMEM((pad_e, 128), jnp.int32),
        pltpu.VMEM((pad_e, 128), jnp.int32),
        pltpu.VMEM((pad_r, width), BF16),
        pltpu.VMEM((owners, 8, 128), F32),
        pltpu.VMEM((owners, 8, 128), F32),
    ]
    used = sum(2 * s.shape[0] * functools.reduce(lambda a, b: a * b, s.shape[1:]) * (s.dtype.itemsize // 2)
               for s in scratch)
    scratch += [
        dma((experts - 1, chunks)), dma((2, chunks)), dma((experts - 1, 2, chunks)), dma((experts, chunks)),
        dma((experts, group)), dma((chunks,)), dma((2,)), dma((owners,)),
        dma((owners, chunks)), dma((owners,)), dma((chunks,)), dma((2,)), dma((owners,)),
        dma((chunks,)), dma((chunks,)), dma((chunks,)),
    ]
    scaled, held_t, hidden_grad, following, router_next, logit = pl.pallas_call(
        functools.partial(exchange, (sections, owners, experts, cap, chunks)),
        out_shape=(
            shape((chunks, slots, CHUNK), BF16),
            shape((hid, slots), BF16),
            shape((slots, hid), BF16),
            shape((chunks, toks, CHUNK), BF16),
            shape((pad_r, width), BF16),
            shape((toks, 128), F32),
        ),
        in_specs=[vmem, smem, vmem, vmem, vmem, anyw, anyw],
        out_specs=(anyw, vmem, vmem, anyw, anyw, vmem),
        scratch_shapes=scratch,
        compiler_params=pltpu.CompilerParams(
            collective_id=0, has_side_effects=True, vmem_limit_bytes=used + 12 * 2**20),
        cost_estimate=pl.CostEstimate(
            flops=2 * slots * hid * width, bytes_accessed=2 * width * (2 * toks + hid + slots),
            transcendentals=0),
    )(slot_token[0, 0], slot_count[0, 0], slot_gate[0, 0], held, router_weight[0].T, grad, w_block)

    down_grad, passed = pl.pallas_call(
        functools.partial(finish, sections, experts),
        grid=(chunks,),
        out_shape=(shape((hid, width), BF16), shape((toks, width), BF16)),
        in_specs=[
            pl.BlockSpec((hid, slots), lambda k: (0, 0)),
            pl.BlockSpec((1, slots, CHUNK), lambda k: (k, 0, 0)),
            pl.BlockSpec((toks, 128), lambda k: (0, 0)),
            pl.BlockSpec((1, toks, CHUNK), lambda k: (k, 0, 0)),
            pl.BlockSpec((pad_r, CHUNK), lambda k: (0, k)),
        ],
        out_specs=(
            pl.BlockSpec((hid, CHUNK), lambda k: (0, k)),
            pl.BlockSpec((toks, CHUNK), lambda k: (0, k)),
        ),
        compiler_params=pltpu.CompilerParams(vmem_limit_bytes=24 * 2**20),
        cost_estimate=pl.CostEstimate(
            flops=2 * slots * hid * width, bytes_accessed=2 * width * (2 * toks + hid + slots),
            transcendentals=0),
    )(held_t, scaled, logit, following, router_next)
    return down_grad[None], hidden_grad.reshape(hidden_saved.shape), passed[None]


def solution(mesh):
    return jax.shard_map(
        shards,
        mesh=mesh,
        in_specs=(
            P("section", "expert", None),
            P("section", None, None),
            P("section", "expert", None),
            P("section", "expert", None, None, None),
            P("section", "expert", None, None),
            P("section", "expert", None),
            P("section", "expert", None, None),
        ),
        out_specs=(
            P("section", "expert", None),
            P("section", "expert", None, None, None),
            P("section", "expert", None),
        ),
        check_vma=False,
    )
```

```python
import functools

import jax
import jax.numpy as jnp
from jax import lax
from jax.experimental import pallas as pl
from jax.experimental.pallas import tpu as pltpu
from jax.sharding import PartitionSpec as P

MESH = pl.DeviceIdType.MESH
F32 = jnp.float32
BF16 = jnp.bfloat16
CHUNK = 512
LEAD = 2


def exchange(
    sizes,
    tok_hbm, cnt_hbm, gate_hbm, held_hbm, router_hbm, grad_hbm, w_hbm,
    scaled_hbm, held_t_ref, hg_ref, next_hbm, rnext_hbm, logit_ref,
    tok_ref, cnt_ref, gate_ref, held_ref, router_ref,
    gradv, wv, buf, outbuf, scaledv, proj, onehot, gsend, grecv, gcol,
    tsend, trecv, rsend, psend, precv,
    s_out, s_own, s_fwd, s_diag, s_gate, s_next, s_small, s_part,
    r_blk, r_gate, r_next, r_small, r_part, l_grad, l_w, l_scaled, l_in,
):
    sections, owners, experts, cap, chunks = sizes
    group = owners // experts
    width = gradv.shape[2]
    toks = gradv.shape[1]
    sec = lax.axis_index("section")
    me = lax.axis_index("expert")
    mine = me // group
    member = lax.rem(me, group)
    hi, lo = member // 2, lax.rem(member, 2)
    far_m = (1 - hi) * 2 + lo
    side_m = hi * 2 + (1 - lo)
    diag_m = (1 - hi) * 2 + (1 - lo)

    def at_expert(index):
        return {"section": sec, "expert": index}

    def at_previous(index):
        return {"section": sec - 1, "expert": index}

    def in_group(r, m):
        return lax.rem(mine + r, experts) * group + m

    def block(source, c):
        return buf.at[c, pl.ds(pl.multiple_of(source * cap, cap), cap)]

    def grad_load(c):
        return pltpu.make_async_copy(
            grad_hbm.at[:, pl.ds(pl.multiple_of(c * width, width), width)], gradv.at[c], l_grad.at[c])

    def w_load(c):
        return pltpu.make_async_copy(
            w_hbm.at[:, pl.ds(pl.multiple_of(c * width, width), width)], wv.at[c], l_w.at[c])

    def scaled_store(c):
        return pltpu.make_async_copy(scaledv.at[c], scaled_hbm.at[c], l_scaled.at[c])

    def send(src, dst, s_sem, r_sem, device):
        return pltpu.make_async_remote_copy(
            src_ref=src, dst_ref=dst, send_sem=s_sem, recv_sem=r_sem,
            device_id=device, device_id_type=MESH)

    def out_copy(r, c):
        return send(outbuf.at[r - 1, c], block(me, c), s_out.at[r - 1, c], r_blk.at[me, c],
                    at_expert(in_group(r, member)))

    def relay(source, c, s_sem, m):
        return send(block(source, c), block(source, c), s_sem, r_blk.at[source, c],
                    at_expert(in_group(0, m)))

    def own_copy(side, c):
        return relay(me, c, s_own.at[side, c], side_m if side else far_m)

    def fwd_copy(r, side, c):
        return relay(in_group(r, member), c, s_fwd.at[r - 1, side, c], side_m if side else far_m)

    def diag_by_far(r, c):
        return relay(in_group(r, far_m), c, s_diag.at[r, c], side_m)

    def diag_by_side(r, c):
        return relay(in_group(r, side_m), c, s_diag.at[r, c], far_m)

    def got(source, c):
        relay(source, c, s_own.at[0, c], far_m).wait_recv()

    def next_copy(c):
        return send(gradv.at[c], next_hbm.at[c], s_next.at[c], r_next.at[c], at_previous(me))

    def router_copy():
        return send(rsend, rnext_hbm, s_small.at[0], r_small.at[0], at_previous(me))

    def token_copy():
        return send(tsend, trecv, s_small.at[1], r_small.at[1], at_previous(me))

    def gate_copy(r, q):
        return send(gsend.at[r], grecv.at[me], s_gate.at[r, q], r_gate.at[me],
                    at_expert(in_group(r, lax.rem(member + q, group))))

    def part_copy(i):
        return send(psend.at[i], precv.at[me], s_part.at[i], r_part.at[me], at_previous(i))

    gate_pairs = [(r, q) for r in range(experts) for q in range(group) if r or q]

    loads = [
        pltpu.make_async_copy(src, dst, l_in.at[i])
        for i, (src, dst) in enumerate((
            (tok_hbm, tok_ref), (cnt_hbm, cnt_ref), (gate_hbm, gate_ref),
            (router_hbm, router_ref), (held_hbm, held_ref)))
    ]
    for load in loads[:3]:
        load.start()
    grad_load(0).start()
    for load in loads[3:]:
        load.start()

    barrier = pltpu.get_barrier_semaphore()
    for step in range(1, owners):
        pl.semaphore_signal(barrier, inc=1, device_id=at_expert(lax.rem(me + step, owners)),
                            device_id_type=MESH)

    @pl.when(sec < sections - 1)
    def _():
        for i in range(owners):
            pl.semaphore_signal(barrier, inc=1, device_id={"section": sec + 1, "expert": i},
                                device_id_type=MESH)

    def start_grad(c, carry):
        grad_load(c).start()
        return carry

    def start_w(c, carry):
        w_load(c).start()
        return carry

    lax.fori_loop(1, chunks, start_grad, 0)
    lax.fori_loop(0, chunks, start_w, 0)

    eye = lax.broadcasted_iota(jnp.int32, (cap, cap), 0) == lax.broadcasted_iota(jnp.int32, (cap, cap), 1)
    slot = lax.broadcasted_iota(jnp.int32, (1, cap), 1)
    for load in loads[:3]:
        load.wait()
    counts = cnt_ref[...].astype(F32)
    entry = lax.broadcasted_iota(jnp.int32, counts.shape, 1)

    def alive(e):
        return slot.astype(F32) < jnp.sum(jnp.where(entry == e, counts, 0.0), axis=1, keepdims=True)

    def column(row):
        return jnp.sum(jnp.where(eye, row, 0.0), axis=1, keepdims=True)

    def row_of(col):
        return jnp.sum(jnp.where(eye, col, 0.0), axis=0, keepdims=True)

    places = lax.broadcasted_iota(jnp.int32, (cap, toks), 1).astype(F32)
    gsend[...] = jnp.zeros_like(gsend)
    tsend[...] = jnp.full(tsend.shape, -1, jnp.int32)
    for r in range(experts):
        e = lax.rem(mine + r, experts)
        live = alive(e)
        tok = jnp.where(live, tok_ref[pl.ds(e, 1), :], -1)
        hit = jnp.where(column(tok.astype(F32)) == places, 1.0, 0.0)
        onehot[r * cap:(r + 1) * cap, :] = hit.astype(BF16)
        gsend[r, 0:1, 0:cap] = jnp.where(live, gate_ref[pl.ds(e, 1), :], 0.0)
    for e in range(experts):
        tsend[e:e + 1, 0:cap] = jnp.where(alive(e), tok_ref[e:e + 1, :], -1)
    grecv[me] = gsend[0]

    def gather(c):
        grad_load(c).wait()
        rows = lax.dot_general(onehot[...], gradv[c], (((1,), (0,)), ((), ())),
                               preferred_element_type=F32).astype(BF16)
        buf[c, pl.ds(pl.multiple_of(me * cap, cap), cap), :] = rows[:cap]
        for r in range(1, experts):
            outbuf[r - 1, c] = rows[r * cap:(r + 1) * cap]

    gather(0)
    rsend[...] = jnp.zeros_like(rsend)
    loads[3].wait()
    rsend[0:experts, :] = router_ref[...]
    pl.semaphore_wait(barrier, (owners - 1) + jnp.where(sec > 0, owners, 0))

    def drain(c):
        for r in range(1, experts):
            out_copy(r, c).wait_send()
            fwd_copy(r, 0, c).wait_send()
            fwd_copy(r, 1, c).wait_send()
        own_copy(0, c).wait_send()
        own_copy(1, c).wait_send()
        for r in range(experts):
            diag_by_far(r, c).wait_send()

        @pl.when(sec > 0)
        def _():
            next_copy(c).wait_send()

        @pl.when(sec < sections - 1)
        def _():
            next_copy(c).wait_recv()

    def step(t, carry):
        @pl.when(t < chunks)
        def _():
            for r in range(1, experts):
                out_copy(r, t).start()
            own_copy(0, t).start()
            own_copy(1, t).start()

            @pl.when(t + 1 < chunks)
            def _():
                gather(t + 1)

            @pl.when(sec > 0)
            def _():
                next_copy(t).start()

        @pl.when(t == 0)
        def _():
            for r, q in gate_pairs:
                gate_copy(r, q).start()

            @pl.when(sec > 0)
            def _():
                router_copy().start()
                token_copy().start()

        c1 = t - LEAD

        @pl.when((c1 >= 0) & (c1 < chunks))
        def _():
            for r in range(1, experts):
                got(in_group(r, member), c1)
                fwd_copy(r, 0, c1).start()
                fwd_copy(r, 1, c1).start()

        c2 = t - 2 * LEAD

        @pl.when((c2 >= 0) & (c2 < chunks))
        def _():
            for r in range(experts):
                got(in_group(r, far_m), c2)
                got(in_group(r, side_m), c2)
                side_first = lax.rem(c2 + 2 * r, 4) == 1

                @pl.when(side_first)
                def _():
                    diag_by_side(r, c2).start()

                @pl.when(jnp.logical_not(side_first))
                def _():
                    diag_by_far(r, c2).start()

        c3 = t - 3 * LEAD

        @pl.when(c3 == 0)
        def _():
            for i in range(1, owners):
                other = lax.rem(me + i, owners)
                send(gsend.at[0], grecv.at[other], s_gate.at[0, 1], r_gate.at[other],
                     at_expert(other)).wait_recv()
            for i in range(owners):
                gcol[i * cap:(i + 1) * cap, :] = jnp.broadcast_to(
                    column(grecv[i, 0:1, 0:cap]), (cap, gcol.shape[1]))
            loads[4].wait()
            held_t_ref[...] = held_ref[...].astype(F32).T.astype(BF16)
            proj[...] = jnp.zeros_like(proj)

        @pl.when(c3 >= 0)
        def _():
            for r in range(experts):
                got(in_group(r, diag_m), c3)
            w_load(c3).wait()
            proj[...] += lax.dot_general(buf[c3], wv[c3], (((1,), (1,)), ((), ())),
                                         preferred_element_type=F32)
            for p in range(0, width, 128):
                scaledv[c3, :, p:p + 128] = (gcol[...] * buf[c3, :, p:p + 128].astype(F32)).astype(BF16)
            scaled_store(c3).start()
            drain(c3)

            @pl.when(c3 > 0)
            def _():
                scaled_store(c3 - 1).wait()

        return carry

    lax.fori_loop(0, chunks + 3 * LEAD, step, 0)

    partial = jnp.sum(held_ref[...].astype(F32) * proj[...], axis=1, keepdims=True)
    psend[...] = jnp.zeros_like(psend)
    for i in range(owners):
        psend[i, 0:1, 0:cap] = row_of(partial[i * cap:(i + 1) * cap])

    @pl.when(sec > 0)
    def _():
        for i in range(owners):
            part_copy(i).start()

    hg_ref[...] = (gcol[:, 0:1] * proj[...]).astype(BF16)

    scaled_store(chunks - 1).wait()
    for r, q in gate_pairs:
        gate_copy(r, q).wait_send()

    logit_ref[...] = jnp.zeros_like(logit_ref)

    @pl.when(sec < sections - 1)
    def _():
        router_copy().wait_recv()
        token_copy().wait_recv()
        for j in range(owners):
            send(psend.at[j], precv.at[j], s_part.at[j], r_part.at[j], at_expert(j)).wait_recv()
        lane = lax.broadcasted_iota(jnp.int32, logit_ref.shape, 1)
        where_tok = lax.broadcasted_iota(jnp.int32, (toks, cap), 0)
        total = jnp.zeros(logit_ref.shape, F32)
        for e in range(experts):
            gate_grad = precv[e * group, 0:1, 0:cap]
            for q in range(1, group):
                gate_grad = gate_grad + precv[e * group + q, 0:1, 0:cap]
            match = where_tok == trecv[e:e + 1, 0:cap]
            col = jnp.sum(jnp.where(match, gate_grad, 0.0), axis=1, keepdims=True)
            total = jnp.where(lane == e, col, total)
        logit_ref[...] = total

    @pl.when(sec > 0)
    def _():
        router_copy().wait_send()
        token_copy().wait_send()
        for i in range(owners):
            part_copy(i).wait_send()


def finish(
    sections, experts, held_t_ref, hg_ref, scaled_ref, logit_ref, next_ref, router_ref,
    down_ref, hidden_ref, passed_ref,
):
    @pl.when(pl.program_id(0) == 0)
    def _():
        hidden_ref[...] = hg_ref[...]

    last = lax.axis_index("section") == sections - 1
    for c in range(scaled_ref.shape[0]):
        cols = slice(c * CHUNK, (c + 1) * CHUNK)
        down_ref[:, cols] = jnp.dot(
            held_t_ref[...], scaled_ref[c], preferred_element_type=F32).astype(BF16)
        total = next_ref[c].astype(F32)
        for e in range(experts):
            total = total + logit_ref[:, e:e + 1] * router_ref[e:e + 1, cols].astype(F32)
        passed_ref[:, cols] = jnp.where(last, 0.0, total).astype(BF16)


def shards(out_grad, router_weight, down_weight, hidden_saved, slot_token, slot_count, slot_gate):
    sections, owners = lax.axis_size("section"), lax.axis_size("expert")
    grad, w_block = out_grad[0], down_weight[0]
    toks, width = grad.shape
    hid = w_block.shape[0]
    experts, cap = slot_token.shape[2:]
    group = owners // experts
    assert group == 4 and width % CHUNK == 0
    chunks = width // CHUNK
    slots = owners * cap
    pad_e = -(-experts // 8) * 8
    pad_r = -(-experts // 16) * 16
    held = hidden_saved.reshape(slots, hid)
    vmem = pl.BlockSpec(memory_space=pltpu.VMEM)
    hbm = pl.BlockSpec(memory_space=pltpu.HBM)
    anyw = pl.BlockSpec(memory_space=pl.ANY)
    dma = pltpu.SemaphoreType.DMA
    shape = jax.ShapeDtypeStruct
    scratch = [
        pltpu.VMEM((experts, cap), jnp.int32),
        pltpu.VMEM((1, experts), jnp.int32),
        pltpu.VMEM((experts, cap), F32),
        pltpu.VMEM((slots, hid), BF16),
        pltpu.VMEM((experts, width), BF16),
        pltpu.VMEM((chunks, toks, CHUNK), BF16),
        pltpu.VMEM((chunks, hid, CHUNK), BF16),
        pltpu.VMEM((chunks, slots, CHUNK), BF16),
        pltpu.VMEM((experts - 1, chunks, cap, CHUNK), BF16),
        pltpu.VMEM((chunks, slots, CHUNK), BF16),
        pltpu.VMEM((slots, hid), F32),
        pltpu.VMEM((experts * cap, toks), BF16),
        pltpu.VMEM((experts, 8, 128), F32),
        pltpu.VMEM((owners, 8, 128), F32),
        pltpu.VMEM((slots, 128), F32),
        pltpu.VMEM((pad_e, 128), jnp.int32),
        pltpu.VMEM((pad_e, 128), jnp.int32),
        pltpu.VMEM((pad_r, width), BF16),
        pltpu.VMEM((owners, 8, 128), F32),
        pltpu.VMEM((owners, 8, 128), F32),
    ]
    scratch += [
        dma((experts - 1, chunks)), dma((2, chunks)), dma((experts - 1, 2, chunks)), dma((experts, chunks)),
        dma((experts, group)), dma((chunks,)), dma((2,)), dma((owners,)),
        dma((owners, chunks)), dma((owners,)), dma((chunks,)), dma((2,)), dma((owners,)),
        dma((chunks,)), dma((chunks,)), dma((chunks,)), dma((5,)),
    ]
    scaled, held_t, hidden_grad, following, router_next, logit = pl.pallas_call(
        functools.partial(exchange, (sections, owners, experts, cap, chunks)),
        out_shape=(
            shape((chunks, slots, CHUNK), BF16),
            shape((hid, slots), BF16),
            shape((slots, hid), BF16),
            shape((chunks, toks, CHUNK), BF16),
            shape((pad_r, width), BF16),
            shape((toks, 128), F32),
        ),
        in_specs=[hbm] * 7,
        out_specs=(anyw, vmem, vmem, anyw, anyw, vmem),
        scratch_shapes=scratch,
        compiler_params=pltpu.CompilerParams(
            collective_id=0, has_side_effects=True, vmem_limit_bytes=64 * 2**20),
        cost_estimate=pl.CostEstimate(
            flops=2 * slots * hid * width, bytes_accessed=2 * width * (2 * toks + hid + slots),
            transcendentals=0),
    )(slot_token[0, 0], slot_count[0], slot_gate[0, 0], held, router_weight[0].T, grad, w_block)

    per = 2 if chunks % 2 == 0 else 1
    down_grad, hidden, passed = pl.pallas_call(
        functools.partial(finish, sections, experts),
        grid=(chunks // per,),
        out_shape=(shape((hid, width), BF16), shape((slots, hid), BF16), shape((toks, width), BF16)),
        in_specs=[
            pl.BlockSpec((hid, slots), lambda k: (0, 0)),
            pl.BlockSpec((slots, hid), lambda k: (0, 0)),
            pl.BlockSpec((per, slots, CHUNK), lambda k: (k, 0, 0)),
            pl.BlockSpec((toks, 128), lambda k: (0, 0)),
            pl.BlockSpec((per, toks, CHUNK), lambda k: (k, 0, 0)),
            pl.BlockSpec((pad_r, per * CHUNK), lambda k: (0, k)),
        ],
        out_specs=(
            pl.BlockSpec((hid, per * CHUNK), lambda k: (0, k)),
            pl.BlockSpec((slots, hid), lambda k: (0, 0)),
            pl.BlockSpec((toks, per * CHUNK), lambda k: (0, k)),
        ),
        compiler_params=pltpu.CompilerParams(vmem_limit_bytes=64 * 2**20),
        cost_estimate=pl.CostEstimate(
            flops=2 * slots * hid * width, bytes_accessed=2 * width * (2 * toks + hid + slots),
            transcendentals=0),
    )(held_t, hidden_grad, scaled, logit, following, router_next)
    return down_grad[None], hidden.reshape(hidden_saved.shape), passed[None]


def solution(mesh):
    return jax.shard_map(
        shards,
        mesh=mesh,
        in_specs=(
            P("section", "expert", None),
            P("section", None, None),
            P("section", "expert", None),
            P("section", "expert", None, None, None),
            P("section", "expert", None, None),
            P("section", "expert", None),
            P("section", "expert", None, None),
        ),
        out_specs=(
            P("section", "expert", None),
            P("section", "expert", None, None, None),
            P("section", "expert", None),
        ),
        check_vma=False,
    )
```

```python
import functools

import jax
import jax.numpy as jnp
from jax import lax
from jax.experimental import pallas as pl
from jax.experimental.pallas import tpu as pltpu
from jax.sharding import PartitionSpec as P

MESH = pl.DeviceIdType.MESH
F32 = jnp.float32
BF16 = jnp.bfloat16
CHUNK = 512
LEAD = 2


def exchange(
    sizes,
    tok_hbm, cnt_hbm, gate_hbm, held_hbm, router_hbm, grad_hbm, w_hbm,
    down_hbm, hg_hbm, next_hbm, rnext_hbm, logit_ref,
    tok_ref, cnt_ref, gate_ref, held_ref, router_ref,
    gradv, wv, buf, outbuf, downv, hgv, held_t, proj, onehot, gsend, grecv, gcol,
    tsend, trecv, rsend, psend, precv,
    s_out, s_own, s_fwd, s_diag, s_gate, s_next, s_small, s_part,
    r_blk, r_gate, r_next, r_small, r_part, l_grad, l_w, l_down, l_in,
):
    sections, owners, experts, cap, chunks = sizes
    group = owners // experts
    width = gradv.shape[2]
    toks = gradv.shape[1]
    sec = lax.axis_index("section")
    me = lax.axis_index("expert")
    mine = me // group
    member = lax.rem(me, group)
    hi, lo = member // 2, lax.rem(member, 2)
    far_m = (1 - hi) * 2 + lo
    side_m = hi * 2 + (1 - lo)
    diag_m = (1 - hi) * 2 + (1 - lo)

    def at_expert(index):
        return {"section": sec, "expert": index}

    def at_previous(index):
        return {"section": sec - 1, "expert": index}

    def in_group(r, m):
        return lax.rem(mine + r, experts) * group + m

    def block(source, c):
        return buf.at[c, pl.ds(pl.multiple_of(source * cap, cap), cap)]

    def grad_load(c):
        return pltpu.make_async_copy(
            grad_hbm.at[:, pl.ds(pl.multiple_of(c * width, width), width)], gradv.at[c], l_grad.at[c])

    def w_load(c):
        return pltpu.make_async_copy(
            w_hbm.at[:, pl.ds(pl.multiple_of(c * width, width), width)], wv.at[c], l_w.at[c])

    def down_store(c):
        return pltpu.make_async_copy(
            downv.at[c], down_hbm.at[:, pl.ds(pl.multiple_of(c * width, width), width)], l_down.at[c])

    def send(src, dst, s_sem, r_sem, device):
        return pltpu.make_async_remote_copy(
            src_ref=src, dst_ref=dst, send_sem=s_sem, recv_sem=r_sem,
            device_id=device, device_id_type=MESH)

    def out_copy(r, c):
        return send(outbuf.at[r - 1, c], block(me, c), s_out.at[r - 1, c], r_blk.at[me, c],
                    at_expert(in_group(r, member)))

    def relay(source, c, s_sem, m):
        return send(block(source, c), block(source, c), s_sem, r_blk.at[source, c],
                    at_expert(in_group(0, m)))

    def own_copy(side, c):
        return relay(me, c, s_own.at[side, c], side_m if side else far_m)

    def fwd_copy(r, side, c):
        return relay(in_group(r, member), c, s_fwd.at[r - 1, side, c], side_m if side else far_m)

    def diag_by_far(r, c):
        return relay(in_group(r, far_m), c, s_diag.at[r, c], side_m)

    def diag_by_side(r, c):
        return relay(in_group(r, side_m), c, s_diag.at[r, c], far_m)

    def got(source, c):
        relay(source, c, s_own.at[0, c], far_m).wait_recv()

    def next_copy(c):
        return send(gradv.at[c], next_hbm.at[c], s_next.at[c], r_next.at[c], at_previous(me))

    def router_copy():
        return send(rsend, rnext_hbm, s_small.at[0], r_small.at[0], at_previous(me))

    def token_copy():
        return send(tsend, trecv, s_small.at[1], r_small.at[1], at_previous(me))

    def gate_copy(r, q):
        return send(gsend.at[r], grecv.at[me], s_gate.at[r, q], r_gate.at[me],
                    at_expert(in_group(r, lax.rem(member + q, group))))

    def part_copy(i):
        return send(psend.at[i], precv.at[me], s_part.at[i], r_part.at[me], at_previous(i))

    gate_pairs = [(r, q) for r in range(experts) for q in range(group) if r or q]

    loads = [
        pltpu.make_async_copy(src, dst, l_in.at[i])
        for i, (src, dst) in enumerate((
            (tok_hbm, tok_ref), (cnt_hbm, cnt_ref), (gate_hbm, gate_ref),
            (router_hbm, router_ref), (held_hbm, held_ref)))
    ]
    for load in loads[:3]:
        load.start()
    grad_load(0).start()
    for load in loads[3:]:
        load.start()

    barrier = pltpu.get_barrier_semaphore()
    for step in range(1, owners):
        pl.semaphore_signal(barrier, inc=1, device_id=at_expert(lax.rem(me + step, owners)),
                            device_id_type=MESH)

    @pl.when(sec < sections - 1)
    def _():
        for i in range(owners):
            pl.semaphore_signal(barrier, inc=1, device_id={"section": sec + 1, "expert": i},
                                device_id_type=MESH)

    def start_grad(c, carry):
        grad_load(c).start()
        return carry

    def start_w(c, carry):
        w_load(c).start()
        return carry

    lax.fori_loop(1, chunks, start_grad, 0)
    lax.fori_loop(0, chunks, start_w, 0)

    eye = lax.broadcasted_iota(jnp.int32, (cap, cap), 0) == lax.broadcasted_iota(jnp.int32, (cap, cap), 1)
    slot = lax.broadcasted_iota(jnp.int32, (1, cap), 1)
    for load in loads[:3]:
        load.wait()
    counts = cnt_ref[...].astype(F32)
    entry = lax.broadcasted_iota(jnp.int32, counts.shape, 1)

    def alive(e):
        return slot.astype(F32) < jnp.sum(jnp.where(entry == e, counts, 0.0), axis=1, keepdims=True)

    def column(row):
        return jnp.sum(jnp.where(eye, row, 0.0), axis=1, keepdims=True)

    def row_of(col):
        return jnp.sum(jnp.where(eye, col, 0.0), axis=0, keepdims=True)

    places = lax.broadcasted_iota(jnp.int32, (cap, toks), 1).astype(F32)
    gsend[...] = jnp.zeros_like(gsend)
    tsend[...] = jnp.full(tsend.shape, -1, jnp.int32)
    for r in range(experts):
        e = lax.rem(mine + r, experts)
        live = alive(e)
        tok = jnp.where(live, tok_ref[pl.ds(e, 1), :], -1)
        hit = jnp.where(column(tok.astype(F32)) == places, 1.0, 0.0)
        onehot[r * cap:(r + 1) * cap, :] = hit.astype(BF16)
        gsend[r, 0:1, 0:cap] = jnp.where(live, gate_ref[pl.ds(e, 1), :], 0.0)
    for e in range(experts):
        tsend[e:e + 1, 0:cap] = jnp.where(alive(e), tok_ref[e:e + 1, :], -1)
    grecv[me] = gsend[0]

    def gather(c):
        grad_load(c).wait()
        rows = lax.dot_general(onehot[...], gradv[c], (((1,), (0,)), ((), ())),
                               preferred_element_type=F32).astype(BF16)
        buf[c, pl.ds(pl.multiple_of(me * cap, cap), cap), :] = rows[:cap]
        for r in range(1, experts):
            outbuf[r - 1, c] = rows[r * cap:(r + 1) * cap]

    gather(0)
    rsend[...] = jnp.zeros_like(rsend)
    loads[3].wait()
    rsend[0:experts, :] = router_ref[...]
    pl.semaphore_wait(barrier, (owners - 1) + jnp.where(sec > 0, owners, 0))

    def drain(c):
        for r in range(1, experts):
            out_copy(r, c).wait_send()
            fwd_copy(r, 0, c).wait_send()
            fwd_copy(r, 1, c).wait_send()
        own_copy(0, c).wait_send()
        own_copy(1, c).wait_send()
        for r in range(experts):
            diag_by_far(r, c).wait_send()

        @pl.when(sec > 0)
        def _():
            next_copy(c).wait_send()

        @pl.when(sec < sections - 1)
        def _():
            next_copy(c).wait_recv()

    def step(t, carry):
        @pl.when(t < chunks)
        def _():
            for r in range(1, experts):
                out_copy(r, t).start()
            own_copy(0, t).start()
            own_copy(1, t).start()

            @pl.when(t + 1 < chunks)
            def _():
                gather(t + 1)

            @pl.when(sec > 0)
            def _():
                next_copy(t).start()

        @pl.when(t == 0)
        def _():
            for r, q in gate_pairs:
                gate_copy(r, q).start()

            @pl.when(sec > 0)
            def _():
                router_copy().start()
                token_copy().start()

        c1 = t - LEAD

        @pl.when((c1 >= 0) & (c1 < chunks))
        def _():
            for r in range(1, experts):
                got(in_group(r, member), c1)
                fwd_copy(r, 0, c1).start()
                fwd_copy(r, 1, c1).start()

        c2 = t - 2 * LEAD

        @pl.when((c2 >= 0) & (c2 < chunks))
        def _():
            for r in range(experts):
                got(in_group(r, far_m), c2)
                got(in_group(r, side_m), c2)
                side_first = lax.rem(c2 + 2 * r, 4) == 1

                @pl.when(side_first)
                def _():
                    diag_by_side(r, c2).start()

                @pl.when(jnp.logical_not(side_first))
                def _():
                    diag_by_far(r, c2).start()

        c3 = t - 3 * LEAD

        @pl.when(c3 == 0)
        def _():
            for i in range(1, owners):
                other = lax.rem(me + i, owners)
                send(gsend.at[0], grecv.at[other], s_gate.at[0, 1], r_gate.at[other],
                     at_expert(other)).wait_recv()
            for i in range(owners):
                gcol[i * cap:(i + 1) * cap, :] = jnp.broadcast_to(
                    column(grecv[i, 0:1, 0:cap]), (cap, gcol.shape[1]))
            loads[4].wait()
            held_t[...] = held_ref[...].astype(F32).T.astype(BF16)
            proj[...] = jnp.zeros_like(proj)

        @pl.when(c3 >= 0)
        def _():
            for r in range(experts):
                got(in_group(r, diag_m), c3)
            w_load(c3).wait()
            proj[...] += lax.dot_general(buf[c3], wv[c3], (((1,), (1,)), ((), ())),
                                         preferred_element_type=F32)
            scaled = jnp.concatenate(
                [(gcol[...] * buf[c3, :, p:p + 128].astype(F32)).astype(BF16) for p in range(0, width, 128)],
                axis=1)
            downv[c3] = jnp.dot(held_t[...], scaled, preferred_element_type=F32).astype(BF16)
            down_store(c3).start()
            drain(c3)

            @pl.when(c3 > 0)
            def _():
                down_store(c3 - 1).wait()

        return carry

    lax.fori_loop(0, chunks + 3 * LEAD, step, 0)

    partial = jnp.sum(held_ref[...].astype(F32) * proj[...], axis=1, keepdims=True)
    psend[...] = jnp.zeros_like(psend)
    for i in range(owners):
        psend[i, 0:1, 0:cap] = row_of(partial[i * cap:(i + 1) * cap])

    @pl.when(sec > 0)
    def _():
        for i in range(owners):
            part_copy(i).start()

    hgv[...] = (gcol[:, 0:1] * proj[...]).astype(BF16)

    hg_store = pltpu.make_async_copy(hgv, hg_hbm, l_in.at[0])
    hg_store.start()
    down_store(chunks - 1).wait()
    hg_store.wait()
    for r, q in gate_pairs:
        gate_copy(r, q).wait_send()

    logit_ref[...] = jnp.zeros_like(logit_ref)

    @pl.when(sec < sections - 1)
    def _():
        router_copy().wait_recv()
        token_copy().wait_recv()
        for j in range(owners):
            send(psend.at[j], precv.at[j], s_part.at[j], r_part.at[j], at_expert(j)).wait_recv()
        lane = lax.broadcasted_iota(jnp.int32, logit_ref.shape, 1)
        where_tok = lax.broadcasted_iota(jnp.int32, (toks, cap), 0)
        total = jnp.zeros(logit_ref.shape, F32)
        for e in range(experts):
            gate_grad = precv[e * group, 0:1, 0:cap]
            for q in range(1, group):
                gate_grad = gate_grad + precv[e * group + q, 0:1, 0:cap]
            match = where_tok == trecv[e:e + 1, 0:cap]
            col = jnp.sum(jnp.where(match, gate_grad, 0.0), axis=1, keepdims=True)
            total = jnp.where(lane == e, col, total)
        logit_ref[...] = total

    @pl.when(sec > 0)
    def _():
        router_copy().wait_send()
        token_copy().wait_send()
        for i in range(owners):
            part_copy(i).wait_send()


def finish(
    sections, experts,
    down_in, hg_in, next_in, router_ref, logit_ref,
    down_out, hg_out, passed_out,
    nextv, passv, l_next, l_pass, l_down, l_hg,
):
    chunks, toks, width = nextv.shape
    pieces = l_down.shape[0]
    rows = down_in.shape[0] // pieces

    def load(c):
        return pltpu.make_async_copy(next_in.at[c], nextv.at[c], l_next.at[c])

    def store(c):
        return pltpu.make_async_copy(
            passv.at[c], passed_out.at[:, pl.ds(pl.multiple_of(c * width, width), width)], l_pass.at[c])

    def move(i):
        part = pl.ds(pl.multiple_of(i * rows, rows), rows)
        return pltpu.make_async_copy(down_in.at[part], down_out.at[part], l_down.at[i])

    def each(count, act):
        def body(i, carry):
            act(i)
            return carry

        lax.fori_loop(0, count, body, 0)

    each(chunks, lambda c: load(c).start())
    each(pieces, lambda i: move(i).start())
    hg_move = pltpu.make_async_copy(hg_in, hg_out, l_hg.at[0])
    hg_move.start()
    last = lax.axis_index("section") == sections - 1

    def form(c):
        load(c).wait()
        total = nextv[c].astype(F32)
        cols = pl.ds(pl.multiple_of(c * width, width), width)
        routers = router_ref[:, cols].astype(F32)
        for e in range(experts):
            total = total + logit_ref[:, e:e + 1] * routers[e:e + 1]
        passv[c] = jnp.where(last, 0.0, total).astype(BF16)
        store(c).start()

    each(chunks, form)
    each(chunks, lambda c: store(c).wait())
    each(pieces, lambda i: move(i).wait())
    hg_move.wait()


def shards(out_grad, router_weight, down_weight, hidden_saved, slot_token, slot_count, slot_gate):
    sections, owners = lax.axis_size("section"), lax.axis_size("expert")
    grad, w_block = out_grad[0], down_weight[0]
    toks, width = grad.shape
    hid = w_block.shape[0]
    experts, cap = slot_token.shape[2:]
    group = owners // experts
    assert group == 4 and width % CHUNK == 0
    chunks = width // CHUNK
    slots = owners * cap
    pad_e = -(-experts // 8) * 8
    pad_r = -(-experts // 16) * 16
    held = hidden_saved.reshape(slots, hid)
    vmem = pl.BlockSpec(memory_space=pltpu.VMEM)
    hbm = pl.BlockSpec(memory_space=pltpu.HBM)
    anyw = pl.BlockSpec(memory_space=pl.ANY)
    dma = pltpu.SemaphoreType.DMA
    shape = jax.ShapeDtypeStruct
    scratch = [
        pltpu.VMEM((experts, cap), jnp.int32),
        pltpu.VMEM((1, experts), jnp.int32),
        pltpu.VMEM((experts, cap), F32),
        pltpu.VMEM((slots, hid), BF16),
        pltpu.VMEM((experts, width), BF16),
        pltpu.VMEM((chunks, toks, CHUNK), BF16),
        pltpu.VMEM((chunks, hid, CHUNK), BF16),
        pltpu.VMEM((chunks, slots, CHUNK), BF16),
        pltpu.VMEM((experts - 1, chunks, cap, CHUNK), BF16),
        pltpu.VMEM((chunks, hid, CHUNK), BF16),
        pltpu.VMEM((slots, hid), BF16),
        pltpu.VMEM((hid, slots), BF16),
        pltpu.VMEM((slots, hid), F32),
        pltpu.VMEM((experts * cap, toks), BF16),
        pltpu.VMEM((experts, 8, 128), F32),
        pltpu.VMEM((owners, 8, 128), F32),
        pltpu.VMEM((slots, 128), F32),
        pltpu.VMEM((pad_e, 128), jnp.int32),
        pltpu.VMEM((pad_e, 128), jnp.int32),
        pltpu.VMEM((pad_r, width), BF16),
        pltpu.VMEM((owners, 8, 128), F32),
        pltpu.VMEM((owners, 8, 128), F32),
    ]
    scratch += [
        dma((experts - 1, chunks)), dma((2, chunks)), dma((experts - 1, 2, chunks)), dma((experts, chunks)),
        dma((experts, group)), dma((chunks,)), dma((2,)), dma((owners,)),
        dma((owners, chunks)), dma((owners,)), dma((chunks,)), dma((2,)), dma((owners,)),
        dma((chunks,)), dma((chunks,)), dma((chunks,)), dma((5,)),
    ]
    down_grad, hidden_grad, following, router_next, logit = pl.pallas_call(
        functools.partial(exchange, (sections, owners, experts, cap, chunks)),
        out_shape=(
            shape((hid, width), BF16),
            shape((slots, hid), BF16),
            shape((chunks, toks, CHUNK), BF16),
            shape((pad_r, width), BF16),
            shape((toks, 128), F32),
        ),
        in_specs=[hbm] * 7,
        out_specs=(anyw, anyw, anyw, anyw, vmem),
        scratch_shapes=scratch,
        compiler_params=pltpu.CompilerParams(
            collective_id=0, has_side_effects=True, vmem_limit_bytes=64 * 2**20),
        cost_estimate=pl.CostEstimate(
            flops=4 * slots * hid * width, bytes_accessed=2 * width * (2 * toks + hid + slots),
            transcendentals=0),
    )(slot_token[0, 0], slot_count[0], slot_gate[0, 0], held, router_weight[0].T, grad, w_block)

    down_grad, hidden, passed = pl.pallas_call(
        functools.partial(finish, sections, experts),
        out_shape=(shape((hid, width), BF16), shape((slots, hid), BF16), shape((toks, width), BF16)),
        in_specs=[anyw, anyw, anyw, vmem, vmem],
        out_specs=(anyw, anyw, anyw),
        scratch_shapes=[
            pltpu.VMEM((chunks, toks, CHUNK), BF16),
            pltpu.VMEM((chunks, toks, CHUNK), BF16),
            dma((chunks,)), dma((chunks,)), dma((8,)), dma((1,)),
        ],
        compiler_params=pltpu.CompilerParams(vmem_limit_bytes=64 * 2**20),
        cost_estimate=pl.CostEstimate(
            flops=2 * toks * experts * width, bytes_accessed=4 * width * (toks + hid),
            transcendentals=0),
    )(down_grad, hidden_grad, following, router_next, logit)
    return down_grad[None], hidden.reshape(hidden_saved.shape), passed[None]


def solution(mesh):
    return jax.shard_map(
        shards,
        mesh=mesh,
        in_specs=(
            P("section", "expert", None),
            P("section", None, None),
            P("section", "expert", None),
            P("section", "expert", None, None, None),
            P("section", "expert", None, None),
            P("section", "expert", None),
            P("section", "expert", None, None),
        ),
        out_specs=(
            P("section", "expert", None),
            P("section", "expert", None, None, None),
            P("section", "expert", None),
        ),
        check_vma=False,
    )
```

```python
import functools

import jax
import jax.numpy as jnp
from jax import lax
from jax.experimental import pallas as pl
from jax.experimental.pallas import tpu as pltpu
from jax.sharding import PartitionSpec as P

MESH = pl.DeviceIdType.MESH
F32 = jnp.float32
BF16 = jnp.bfloat16
CHUNK = 512
LEAD = 2


def exchange(
    sizes,
    tok_hbm, cnt_hbm, gate_hbm, held_hbm, router_hbm, grad_hbm, w_hbm,
    down_hbm, hg_hbm, next_hbm, rnext_hbm, logit_ref,
    tok_ref, cnt_ref, gate_ref, held_ref, router_ref,
    gradv, wv, buf, outbuf, downv, hgv, held_t, proj, onehot, gsend, grecv, gcol,
    tsend, trecv, rsend, psend, precv,
    s_out, s_own, s_fwd, s_diag, s_gate, s_next, s_small, s_part,
    r_blk, r_gate, r_next, r_small, r_part, l_grad, l_w, l_down, l_in,
):
    sections, owners, experts, cap, chunks = sizes
    group = owners // experts
    width = gradv.shape[2]
    toks = gradv.shape[1]
    sec = lax.axis_index("section")
    me = lax.axis_index("expert")
    mine = me // group
    member = lax.rem(me, group)
    hi, lo = member // 2, lax.rem(member, 2)
    far_m = (1 - hi) * 2 + lo
    side_m = hi * 2 + (1 - lo)
    diag_m = (1 - hi) * 2 + (1 - lo)

    def at_expert(index):
        return {"section": sec, "expert": index}

    def at_previous(index):
        return {"section": sec - 1, "expert": index}

    def in_group(r, m):
        return lax.rem(mine + r, experts) * group + m

    def block(source, c):
        return buf.at[c, pl.ds(pl.multiple_of(source * cap, cap), cap)]

    def grad_load(c):
        return pltpu.make_async_copy(
            grad_hbm.at[:, pl.ds(pl.multiple_of(c * width, width), width)], gradv.at[c], l_grad.at[c])

    def w_load(c):
        return pltpu.make_async_copy(
            w_hbm.at[:, pl.ds(pl.multiple_of(c * width, width), width)], wv.at[c], l_w.at[c])

    def down_store(c):
        return pltpu.make_async_copy(
            downv.at[c], down_hbm.at[:, pl.ds(pl.multiple_of(c * width, width), width)], l_down.at[c])

    def send(src, dst, s_sem, r_sem, device):
        return pltpu.make_async_remote_copy(
            src_ref=src, dst_ref=dst, send_sem=s_sem, recv_sem=r_sem,
            device_id=device, device_id_type=MESH)

    def out_copy(r, c):
        return send(outbuf.at[r - 1, c], block(me, c), s_out.at[r - 1, c], r_blk.at[me, c],
                    at_expert(in_group(r, member)))

    def relay(source, c, s_sem, m):
        return send(block(source, c), block(source, c), s_sem, r_blk.at[source, c],
                    at_expert(in_group(0, m)))

    def own_copy(side, c):
        return relay(me, c, s_own.at[side, c], side_m if side else far_m)

    def fwd_copy(r, side, c):
        return relay(in_group(r, member), c, s_fwd.at[r - 1, side, c], side_m if side else far_m)

    def diag_by_far(r, c):
        return relay(in_group(r, far_m), c, s_diag.at[r, c], side_m)

    def diag_by_side(r, c):
        return relay(in_group(r, side_m), c, s_diag.at[r, c], far_m)

    def got(source, c):
        relay(source, c, s_own.at[0, c], far_m).wait_recv()

    def next_copy(c):
        return send(gradv.at[c], next_hbm.at[c], s_next.at[c], r_next.at[c], at_previous(me))

    def router_copy():
        return send(rsend, rnext_hbm, s_small.at[0], r_small.at[0], at_previous(me))

    def token_copy():
        return send(tsend, trecv, s_small.at[1], r_small.at[1], at_previous(me))

    def gate_copy(r, q):
        return send(gsend.at[r], grecv.at[me], s_gate.at[r, q], r_gate.at[me],
                    at_expert(in_group(r, lax.rem(member + q, group))))

    def part_copy(i):
        return send(psend.at[i], precv.at[me], s_part.at[i], r_part.at[me], at_previous(i))

    gate_pairs = [(r, q) for r in range(experts) for q in range(group) if r or q]

    loads = [
        pltpu.make_async_copy(src, dst, l_in.at[i])
        for i, (src, dst) in enumerate((
            (tok_hbm, tok_ref), (cnt_hbm, cnt_ref), (gate_hbm, gate_ref),
            (router_hbm, router_ref), (held_hbm, held_ref)))
    ]
    for load in loads[:3]:
        load.start()
    grad_load(0).start()
    for load in loads[3:]:
        load.start()

    barrier = pltpu.get_barrier_semaphore()
    for step in range(1, owners):
        pl.semaphore_signal(barrier, inc=1, device_id=at_expert(lax.rem(me + step, owners)),
                            device_id_type=MESH)

    @pl.when(sec < sections - 1)
    def _():
        for i in range(owners):
            pl.semaphore_signal(barrier, inc=1, device_id={"section": sec + 1, "expert": i},
                                device_id_type=MESH)

    def start_grad(c, carry):
        grad_load(c).start()
        return carry

    def start_w(c, carry):
        w_load(c).start()
        return carry

    lax.fori_loop(1, chunks, start_grad, 0)
    lax.fori_loop(0, chunks, start_w, 0)

    eye = lax.broadcasted_iota(jnp.int32, (cap, cap), 0) == lax.broadcasted_iota(jnp.int32, (cap, cap), 1)
    slot = lax.broadcasted_iota(jnp.int32, (1, cap), 1)
    for load in loads[:3]:
        load.wait()
    counts = cnt_ref[...].astype(F32)
    entry = lax.broadcasted_iota(jnp.int32, counts.shape, 1)

    def alive(e):
        return slot.astype(F32) < jnp.sum(jnp.where(entry == e, counts, 0.0), axis=1, keepdims=True)

    def column(row):
        return jnp.sum(jnp.where(eye, row, 0.0), axis=1, keepdims=True)

    def row_of(col):
        return jnp.sum(jnp.where(eye, col, 0.0), axis=0, keepdims=True)

    places = lax.broadcasted_iota(jnp.int32, (cap, toks), 1).astype(F32)
    gsend[...] = jnp.zeros_like(gsend)
    tsend[...] = jnp.full(tsend.shape, -1, jnp.int32)
    for r in range(experts):
        e = lax.rem(mine + r, experts)
        live = alive(e)
        tok = jnp.where(live, tok_ref[pl.ds(e, 1), :], -1)
        hit = jnp.where(column(tok.astype(F32)) == places, 1.0, 0.0)
        onehot[r * cap:(r + 1) * cap, :] = hit.astype(BF16)
        gsend[r, 0:1, 0:cap] = jnp.where(live, gate_ref[pl.ds(e, 1), :], 0.0)
    for e in range(experts):
        tsend[e:e + 1, 0:cap] = jnp.where(alive(e), tok_ref[e:e + 1, :], -1)
    grecv[me] = gsend[0]

    def gather(c):
        grad_load(c).wait()
        rows = lax.dot_general(onehot[...], gradv[c], (((1,), (0,)), ((), ())),
                               preferred_element_type=F32).astype(BF16)
        buf[c, pl.ds(pl.multiple_of(me * cap, cap), cap), :] = rows[:cap]
        for r in range(1, experts):
            outbuf[r - 1, c] = rows[r * cap:(r + 1) * cap]

    gather(0)
    rsend[...] = jnp.zeros_like(rsend)
    loads[3].wait()
    rsend[0:experts, :] = router_ref[...]
    pl.semaphore_wait(barrier, (owners - 1) + jnp.where(sec > 0, owners, 0))

    def drain(c):
        for r in range(1, experts):
            out_copy(r, c).wait_send()
            fwd_copy(r, 0, c).wait_send()
            fwd_copy(r, 1, c).wait_send()
        own_copy(0, c).wait_send()
        own_copy(1, c).wait_send()
        for r in range(experts):
            diag_by_far(r, c).wait_send()

        @pl.when(sec > 0)
        def _():
            next_copy(c).wait_send()

        @pl.when(sec < sections - 1)
        def _():
            next_copy(c).wait_recv()

    def step(t, carry):
        @pl.when(t < chunks)
        def _():
            for r in range(1, experts):
                out_copy(r, t).start()
            own_copy(0, t).start()
            own_copy(1, t).start()

            @pl.when(t + 1 < chunks)
            def _():
                gather(t + 1)

            @pl.when(sec > 0)
            def _():
                next_copy(t).start()

        @pl.when(t == 0)
        def _():
            for r, q in gate_pairs:
                gate_copy(r, q).start()

            @pl.when(sec > 0)
            def _():
                router_copy().start()
                token_copy().start()

        c1 = t - LEAD

        @pl.when((c1 >= 0) & (c1 < chunks))
        def _():
            for r in range(1, experts):
                got(in_group(r, member), c1)
                fwd_copy(r, 0, c1).start()
                fwd_copy(r, 1, c1).start()

        c2 = t - 2 * LEAD

        @pl.when((c2 >= 0) & (c2 < chunks))
        def _():
            for r in range(experts):
                got(in_group(r, far_m), c2)
                got(in_group(r, side_m), c2)
                side_first = lax.rem(c2 + 2 * r, 4) == 1

                @pl.when(side_first)
                def _():
                    diag_by_side(r, c2).start()

                @pl.when(jnp.logical_not(side_first))
                def _():
                    diag_by_far(r, c2).start()

        c3 = t - 3 * LEAD

        @pl.when(c3 == 0)
        def _():
            for i in range(1, owners):
                other = lax.rem(me + i, owners)
                send(gsend.at[0], grecv.at[other], s_gate.at[0, 1], r_gate.at[other],
                     at_expert(other)).wait_recv()
            for i in range(owners):
                gcol[i * cap:(i + 1) * cap, :] = jnp.broadcast_to(
                    column(grecv[i, 0:1, 0:cap]), (cap, gcol.shape[1]))
            loads[4].wait()
            held_t[...] = held_ref[...].astype(F32).T.astype(BF16)
            proj[...] = jnp.zeros_like(proj)

        @pl.when(c3 >= 0)
        def _():
            for r in range(experts):
                got(in_group(r, diag_m), c3)
            w_load(c3).wait()
            proj[...] += lax.dot_general(buf[c3], wv[c3], (((1,), (1,)), ((), ())),
                                         preferred_element_type=F32)
            scaled = jnp.concatenate(
                [(gcol[...] * buf[c3, :, p:p + 128].astype(F32)).astype(BF16) for p in range(0, width, 128)],
                axis=1)
            downv[c3] = jnp.dot(held_t[...], scaled, preferred_element_type=F32).astype(BF16)
            down_store(c3).start()
            drain(c3)

            @pl.when(c3 > 0)
            def _():
                down_store(c3 - 1).wait()

        return carry

    lax.fori_loop(0, chunks + 3 * LEAD, step, 0)

    partial = jnp.sum(held_ref[...].astype(F32) * proj[...], axis=1, keepdims=True)
    psend[...] = jnp.zeros_like(psend)
    for i in range(owners):
        psend[i, 0:1, 0:cap] = row_of(partial[i * cap:(i + 1) * cap])

    @pl.when(sec > 0)
    def _():
        for i in range(owners):
            part_copy(i).start()

    hgv[...] = (gcol[:, 0:1] * proj[...]).astype(BF16)

    hg_store = pltpu.make_async_copy(hgv, hg_hbm, l_in.at[0])
    hg_store.start()
    down_store(chunks - 1).wait()
    hg_store.wait()
    for r, q in gate_pairs:
        gate_copy(r, q).wait_send()

    logit_ref[...] = jnp.zeros_like(logit_ref)

    @pl.when(sec < sections - 1)
    def _():
        router_copy().wait_recv()
        token_copy().wait_recv()
        for j in range(owners):
            send(psend.at[j], precv.at[j], s_part.at[j], r_part.at[j], at_expert(j)).wait_recv()
        lane = lax.broadcasted_iota(jnp.int32, logit_ref.shape, 1)
        where_tok = lax.broadcasted_iota(jnp.int32, (toks, cap), 0)
        total = jnp.zeros(logit_ref.shape, F32)
        for e in range(experts):
            gate_grad = precv[e * group, 0:1, 0:cap]
            for q in range(1, group):
                gate_grad = gate_grad + precv[e * group + q, 0:1, 0:cap]
            match = where_tok == trecv[e:e + 1, 0:cap]
            col = jnp.sum(jnp.where(match, gate_grad, 0.0), axis=1, keepdims=True)
            total = jnp.where(lane == e, col, total)
        logit_ref[...] = total

    @pl.when(sec > 0)
    def _():
        router_copy().wait_send()
        token_copy().wait_send()
        for i in range(owners):
            part_copy(i).wait_send()


def finish(
    sections, experts,
    down_in, hg_in, next_in, router_ref, logit_ref,
    down_out, hg_out, passed_out,
    nextv, passv, downv, hgv, l_next, l_pass, l_down, l_out, l_hg,
):
    chunks, toks, width = nextv.shape
    pieces = l_down.shape[0]
    rows = down_in.shape[0] // pieces

    def load(c):
        return pltpu.make_async_copy(next_in.at[c], nextv.at[c], l_next.at[c])

    def store(c):
        return pltpu.make_async_copy(
            passv.at[c], passed_out.at[:, pl.ds(pl.multiple_of(c * width, width), width)], l_pass.at[c])

    def move(i):
        part = pl.ds(pl.multiple_of(i * rows, rows), rows)
        return pltpu.make_async_copy(down_in.at[part], downv.at[part], l_down.at[i])

    def put(i):
        part = pl.ds(pl.multiple_of(i * rows, rows), rows)
        return pltpu.make_async_copy(downv.at[part], down_out.at[part], l_out.at[i])

    def pass_on(i):
        move(i).wait()
        put(i).start()

    def each(count, act):
        def body(i, carry):
            act(i)
            return carry

        lax.fori_loop(0, count, body, 0)

    each(pieces, lambda i: move(i).start())
    each(chunks, lambda c: load(c).start())
    hg_move = pltpu.make_async_copy(hg_in, hgv, l_hg.at[0])
    hg_put = pltpu.make_async_copy(hgv, hg_out, l_hg.at[1])
    hg_move.start()
    each(pieces, pass_on)
    last = lax.axis_index("section") == sections - 1

    def form(c):
        load(c).wait()
        total = nextv[c].astype(F32)
        cols = pl.ds(pl.multiple_of(c * width, width), width)
        routers = router_ref[:, cols].astype(F32)
        for e in range(experts):
            total = total + logit_ref[:, e:e + 1] * routers[e:e + 1]
        passv[c] = jnp.where(last, 0.0, total).astype(BF16)
        store(c).start()

    each(chunks, form)
    hg_move.wait()
    hg_put.start()
    each(chunks, lambda c: store(c).wait())
    each(pieces, lambda i: put(i).wait())
    hg_put.wait()


def shards(out_grad, router_weight, down_weight, hidden_saved, slot_token, slot_count, slot_gate):
    sections, owners = lax.axis_size("section"), lax.axis_size("expert")
    grad, w_block = out_grad[0], down_weight[0]
    toks, width = grad.shape
    hid = w_block.shape[0]
    experts, cap = slot_token.shape[2:]
    group = owners // experts
    assert group == 4 and width % CHUNK == 0
    chunks = width // CHUNK
    slots = owners * cap
    pad_e = -(-experts // 8) * 8
    pad_r = -(-experts // 16) * 16
    held = hidden_saved.reshape(slots, hid)
    vmem = pl.BlockSpec(memory_space=pltpu.VMEM)
    hbm = pl.BlockSpec(memory_space=pltpu.HBM)
    anyw = pl.BlockSpec(memory_space=pl.ANY)
    dma = pltpu.SemaphoreType.DMA
    shape = jax.ShapeDtypeStruct
    scratch = [
        pltpu.VMEM((experts, cap), jnp.int32),
        pltpu.VMEM((1, experts), jnp.int32),
        pltpu.VMEM((experts, cap), F32),
        pltpu.VMEM((slots, hid), BF16),
        pltpu.VMEM((experts, width), BF16),
        pltpu.VMEM((chunks, toks, CHUNK), BF16),
        pltpu.VMEM((chunks, hid, CHUNK), BF16),
        pltpu.VMEM((chunks, slots, CHUNK), BF16),
        pltpu.VMEM((experts - 1, chunks, cap, CHUNK), BF16),
        pltpu.VMEM((chunks, hid, CHUNK), BF16),
        pltpu.VMEM((slots, hid), BF16),
        pltpu.VMEM((hid, slots), BF16),
        pltpu.VMEM((slots, hid), F32),
        pltpu.VMEM((experts * cap, toks), BF16),
        pltpu.VMEM((experts, 8, 128), F32),
        pltpu.VMEM((owners, 8, 128), F32),
        pltpu.VMEM((slots, 128), F32),
        pltpu.VMEM((pad_e, 128), jnp.int32),
        pltpu.VMEM((pad_e, 128), jnp.int32),
        pltpu.VMEM((pad_r, width), BF16),
        pltpu.VMEM((owners, 8, 128), F32),
        pltpu.VMEM((owners, 8, 128), F32),
    ]
    scratch += [
        dma((experts - 1, chunks)), dma((2, chunks)), dma((experts - 1, 2, chunks)), dma((experts, chunks)),
        dma((experts, group)), dma((chunks,)), dma((2,)), dma((owners,)),
        dma((owners, chunks)), dma((owners,)), dma((chunks,)), dma((2,)), dma((owners,)),
        dma((chunks,)), dma((chunks,)), dma((chunks,)), dma((5,)),
    ]
    down_grad, hidden_grad, following, router_next, logit = pl.pallas_call(
        functools.partial(exchange, (sections, owners, experts, cap, chunks)),
        out_shape=(
            shape((hid, width), BF16),
            shape((slots, hid), BF16),
            shape((chunks, toks, CHUNK), BF16),
            shape((pad_r, width), BF16),
            shape((toks, 128), F32),
        ),
        in_specs=[hbm] * 7,
        out_specs=(anyw, anyw, anyw, anyw, vmem),
        scratch_shapes=scratch,
        compiler_params=pltpu.CompilerParams(
            collective_id=0, has_side_effects=True, vmem_limit_bytes=64 * 2**20),
        cost_estimate=pl.CostEstimate(
            flops=4 * slots * hid * width, bytes_accessed=2 * width * (2 * toks + hid + slots),
            transcendentals=0),
    )(slot_token[0, 0], slot_count[0], slot_gate[0, 0], held, router_weight[0].T, grad, w_block)

    down_grad, hidden, passed = pl.pallas_call(
        functools.partial(finish, sections, experts),
        out_shape=(shape((hid, width), BF16), shape((slots, hid), BF16), shape((toks, width), BF16)),
        in_specs=[anyw, anyw, anyw, vmem, vmem],
        out_specs=(anyw, anyw, anyw),
        scratch_shapes=[
            pltpu.VMEM((chunks, toks, CHUNK), BF16),
            pltpu.VMEM((chunks, toks, CHUNK), BF16),
            pltpu.VMEM((hid, width), BF16),
            pltpu.VMEM((slots, hid), BF16),
            dma((chunks,)), dma((chunks,)), dma((8,)), dma((8,)), dma((2,)),
        ],
        compiler_params=pltpu.CompilerParams(vmem_limit_bytes=64 * 2**20),
        cost_estimate=pl.CostEstimate(
            flops=2 * toks * experts * width, bytes_accessed=4 * width * (toks + hid),
            transcendentals=0),
    )(down_grad, hidden_grad, following, router_next, logit)
    return down_grad[None], hidden.reshape(hidden_saved.shape), passed[None]


def solution(mesh):
    return jax.shard_map(
        shards,
        mesh=mesh,
        in_specs=(
            P("section", "expert", None),
            P("section", None, None),
            P("section", "expert", None),
            P("section", "expert", None, None, None),
            P("section", "expert", None, None),
            P("section", "expert", None),
            P("section", "expert", None, None),
        ),
        out_specs=(
            P("section", "expert", None),
            P("section", "expert", None, None, None),
            P("section", "expert", None),
        ),
        check_vma=False,
    )
```
